32 devices in a mesh: groups: 2 (over y), tensor: 4 (over z), dp: 4 (over x, core).
Axes of the slice: x: 2, y: 2, z: 4, core: 2. Of those that a mesh axis runs over, the one named last changes fastest.
Arguments:
- attention: bfloat16 [3, 2048, 8192], P(None, ('groups', 'dp'), 'tensor'), parts along dimension 1, may hold values from -6 to 6
- out_proj: bfloat16 [3, 8192, 8192], P(None, 'tensor', 'dp'), may hold values from -0.0625 to 0.0625
- join_weight: bfloat16 [3, 8192, 8192], P(None, 'dp', 'tensor'), may hold values from -0.0390625 to 0.0390625
- cotangent: bfloat16 [2048, 8192], P(('groups', 'dp'), 'tensor'), parts along dimension 0, may hold values from -0.1875 to 0.1875
- loss_mask: int32 [2048], P(('groups', 'dp')), parts along dimension 0, may hold values 0 or 1
Outputs:
- joined_out: bfloat16 [2048, 8192], P(('groups', 'dp'), 'tensor'), parts along dimension 0
- gradient: bfloat16 [6, 8192, 8192], P('groups', 'dp', 'tensor'), parts along dimension 0
The draws below stay inside these ranges and needn't reach their ends.
There are 2 independent parts, one for each index of `groups`. The reference program is written for one: setup_inputs(seed, part) draws one part's arguments, and reference() takes and returns one part's arrays. A program takes and returns all parts, laid end to end along the dimension named above; an argument that names none is the same for every part. Nothing has to cross between parts.
All inputs are finite; a program needn't handle non-finite values. No bound on the sum of `loss_mask` on one device may be relied on, other than what follows from the above.
Results may differ from the reference program's by a relative error of at most 0.015.
Values may be sent and summed in bfloat16 or wider, within the bound.
No kernel may reach another device: no remote copies, remote signals or barrier semaphores. Data moves between devices by JAX's collectives and lax.ppermute only.
A program may use at most 256 MiB of HBM per device.

```python
import jax
import jax.numpy as jnp
from jax import lax

D = 8192
LAYERS = 3
TOKENS = 1024
N_TENSOR = 4


def place_ends(array, own_key, least, largest):
    dims = array.shape
    spot = [jax.random.randint(jax.random.fold_in(own_key, axis), (), 0, dims[axis]) for axis in range(len(dims))]
    array = array.at[tuple(spot)].set(least)
    longest = dims.index(max(dims))
    spot[longest] = (spot[longest] + 1) % dims[longest]
    return array.at[tuple(spot)].set(largest)


def block_levels(own_key, extent, pieces, low, largest):
    def one(position, parts):
        heights = jax.random.uniform(jax.random.fold_in(jax.random.fold_in(own_key, 6), position), (parts,), jnp.float32, low / len(pieces), largest / len(pieces))
        return jnp.repeat(jnp.exp(heights), extent[position] // parts).reshape((-1,) + (1,) * (len(extent) - position - 1))

    level = one(*pieces[0])
    for cut in pieces[1:]:
        level = level * one(*cut)
    return level


def bell_draw(rng, shape, scale, most, cuts=(), kind=jnp.bfloat16):
    entries = scale * jax.random.normal(rng, shape, jnp.float32)
    if cuts:
        entries = entries * block_levels(rng, shape, cuts, -0.22, 0.18)
    return jnp.clip(entries, -most, most).astype(kind)


def setup_inputs(seed: int = 0, part: int = 0) -> dict:
    seeds = jax.random.split(jax.random.key(seed), 6)
    part_keys = jax.random.split(jax.random.fold_in(seeds[5], part), 6)
    return {
        "attention": bell_draw(part_keys[0], (LAYERS, TOKENS, D), 1.0, 6.0, ((1, 4), (2, 4))),
        "out_proj": bell_draw(seeds[1], (LAYERS, D, D), D ** -0.5, 0.0625, ((1, 4), (2, 4))),
        "join_weight": bell_draw(seeds[2], (LAYERS, D, D), (LAYERS * D) ** -0.5, 0.0390625, ((1, 4), (2, 4))),
        "cotangent": bell_draw(part_keys[3], (TOKENS, D), TOKENS ** -0.5, 0.1875, ((0, 4), (1, 4))),
        "loss_mask": place_ends((jax.random.randint(part_keys[4], (TOKENS,), 0, 4) < 3).astype(jnp.int32), jax.random.fold_in(part_keys[4], 1), 0, 1),
    }


def layer_features(attention_level, proj_level):
    width_block = D // N_TENSOR

    def add_block(piece_index, total):
        offset = piece_index.astype(jnp.int32) * width_block
        left = lax.dynamic_slice_in_dim(attention_level, offset, width_block, 1)
        right = lax.dynamic_slice_in_dim(proj_level, offset, width_block, 0)
        rounded = jnp.dot(left, right, preferred_element_type=jnp.float32).astype(jnp.bfloat16)
        rounded = lax.optimization_barrier(rounded)
        return total + rounded.astype(jnp.float32)

    starting = jnp.zeros((attention_level.shape[0], proj_level.shape[1]), jnp.float32)
    return lax.fori_loop(0, N_TENSOR, add_block, starting)


def reference(attention, out_proj, join_weight, cotangent, loss_mask):
    features = []
    for level in range(LAYERS):
        features.append(layer_features(attention[level], out_proj[level]).astype(jnp.bfloat16))
    joined_total = jnp.zeros((attention.shape[1], join_weight.shape[2]), jnp.float32)
    for level in range(LAYERS):
        joined_total = joined_total + jnp.dot(features[level], join_weight[level], preferred_element_type=jnp.float32)
    joined_out = joined_total.astype(jnp.bfloat16)
    masked = cotangent * loss_mask[:, None].astype(jnp.bfloat16)
    gradient = []
    for level in range(LAYERS):
        gradient.append(jnp.dot(features[level].T, masked, preferred_element_type=jnp.float32).astype(jnp.bfloat16))
    return joined_out, jnp.stack(gradient, axis=0)
```

```python
import jax
import jax.numpy as jnp
from jax import lax
from jax.sharding import PartitionSpec as P

F32 = jnp.float32
BF16 = jnp.bfloat16


def plain(attention, out_proj, join_weight, cotangent, loss_mask):
    partial_value = jnp.einsum(
        "lrk,lkc->rlc",
        lax.all_gather(attention, "dp", axis=1, tiled=True),
        out_proj,
        preferred_element_type=F32,
    )
    masked = cotangent * loss_mask[:, None].astype(BF16)
    cotangent_all = lax.all_gather(masked, "dp", axis=0, tiled=True)
    summed = lax.psum(partial_value.astype(BF16), "tensor")
    joined_part = jnp.einsum("rlf,lfc->rc", summed, join_weight, preferred_element_type=F32)
    gradient = jnp.einsum("rlf,rc->lfc", summed, cotangent_all, preferred_element_type=F32)
    joined_out = lax.psum_scatter(joined_part.astype(BF16), "dp", scatter_dimension=0, tiled=True)
    return (joined_out, gradient.astype(BF16))


def dot(a, b):
    return jnp.dot(a, b, preferred_element_type=F32)


def chain(piece, n):
    total = piece.astype(F32)
    for hops in (
        [(s, s + 1) for s in range(n - 1)],
        [(s + 1, s) for s in reversed(range(n - 1))],
    ):
        send = piece
        for hop in hops:
            got = lax.ppermute(send, "tensor", [hop]).astype(F32)
            send = (piece.astype(F32) + got).astype(BF16)
            total = total + got
    return total.astype(BF16)


def chained(n, cuts):
    near = [(i, i ^ 1) for i in range(4)]
    far = [(i, i ^ 2) for i in range(4)]

    def gather(own):
        across = lax.ppermute(own, "dp", far)
        return [own, lax.ppermute(own, "dp", near), across, lax.ppermute(across, "dp", near)]

    def shards(attention, out_proj, join_weight, cotangent, loss_mask):
        layers, rows, _ = attention.shape
        step = rows // cuts
        masked = gather(cotangent * loss_mask[:, None].astype(BF16))
        joined = [None] * 4
        gradient = []
        for level in range(layers):
            last = level == layers - 1
            tokens = gather(attention[level])
            features = [None] * 4
            for j in (3, 2, 1, 0) if last else (0, 1, 2, 3):
                part = dot(tokens[j], out_proj[level]).astype(BF16)
                features[j] = jnp.concatenate(
                    [chain(part[q * step : (q + 1) * step], n) for q in range(cuts)], axis=0
                )
                term = dot(features[j], join_weight[level])
                joined[j] = term if joined[j] is None else joined[j] + term
            gradient.append(
                lax.dot_general(
                    jnp.concatenate(features, axis=0),
                    jnp.concatenate(masked, axis=0),
                    (((0,), (0,)), ((), ())),
                    preferred_element_type=F32,
                ).astype(BF16)
            )
        across = joined[2] + lax.ppermute(joined[3].astype(BF16), "dp", near).astype(F32)
        across = lax.ppermute(across.astype(BF16), "dp", far)
        beside = lax.ppermute(joined[1].astype(BF16), "dp", near)
        out = joined[0] + beside.astype(F32) + across.astype(F32)
        return (out.astype(BF16), jnp.stack(gradient, axis=0))

    return shards


def solution(mesh):
    placed = (
        P(None, ("groups", "dp"), "tensor"),
        P(None, "tensor", "dp"),
        P(None, "dp", "tensor"),
        P(("groups", "dp"), "tensor"),
        P(("groups", "dp")),
    )
    n = mesh.shape["tensor"]
    body = chained(n, 4) if mesh.shape["dp"] == 4 and n <= 8 else plain
    return jax.shard_map(
        body,
        mesh=mesh,
        in_specs=placed,
        out_specs=(P(("groups", "dp"), "tensor"), P("groups", "dp", "tensor")),
        check_vma=False,
    )
```

```python
import jax
import jax.numpy as jnp
from jax import lax
from jax.experimental import pallas as pl
from jax.experimental.pallas import tpu as pltpu
from jax.sharding import PartitionSpec as P

F32 = jnp.float32
BF16 = jnp.bfloat16
TILE = 16


def plain(attention, out_proj, join_weight, cotangent, loss_mask):
    partial_value = jnp.einsum(
        "lrk,lkc->rlc",
        lax.all_gather(attention, "dp", axis=1, tiled=True),
        out_proj,
        preferred_element_type=F32,
    )
    masked = cotangent * loss_mask[:, None].astype(BF16)
    cotangent_all = lax.all_gather(masked, "dp", axis=0, tiled=True)
    summed = lax.psum(partial_value.astype(BF16), "tensor")
    joined_part = jnp.einsum("rlf,lfc->rc", summed, join_weight, preferred_element_type=F32)
    gradient = jnp.einsum("rlf,rc->lfc", summed, cotangent_all, preferred_element_type=F32)
    joined_out = lax.psum_scatter(joined_part.astype(BF16), "dp", scatter_dimension=0, tiled=True)
    return (joined_out, gradient.astype(BF16))


def dot(a, b):
    return jnp.dot(a, b, preferred_element_type=F32)


def tie(x, *after):
    return lax.optimization_barrier((x, *after))[0]


def slot_sums(n, rows, sums, place, feature, after):
    arrays, where = [], {}

    def number(array):
        if id(array) not in where:
            where[id(array)] = len(arrays)
            arrays.append(array)
        return where[id(array)]

    terms = [[[(number(a), row) for a, row in term] for term in one] for one in sums]
    width = arrays[0].shape[1]
    flat = [term for one in terms for term in one]
    sources = len(arrays)
    extra = list(after) + ([feature] if feature is not None else [])
    sends = len(sums) - (place is not None)

    def kernel(*refs):
        given = refs[:sources]
        results = refs[sources + len(extra) : sources + len(extra) + len(sums)]
        held, total, sems, done = refs[sources + len(extra) + len(sums) :]
        me = lax.axis_index("tensor")

        def copy(t, pick):
            array, row = pick
            return pltpu.make_async_copy(given[array].at[pl.ds(row, rows)], held.at[t], sems.at[t])

        for t, term in enumerate(flat):
            if len(set(term)) == 1:
                copy(t, term[0]).start()
        for v in range(n):

            @pl.when(me == v)
            def _(v=v):
                for t, term in enumerate(flat):
                    if len(set(term)) > 1:
                        copy(t, term[v]).start()

        t = 0
        for index, one in enumerate(terms):
            used = list(range(t, t + len(one)))
            t += len(one)
            for u in used:
                copy(u, flat[u][0]).wait()
            target = total if index == sends else results[index]

            def add(i, carry, used=used, target=target):
                block = pl.ds(pl.multiple_of(i * TILE, TILE), TILE)
                value = held[used[0], block].astype(F32)
                for u in used[1:]:
                    value = value + held[u, block].astype(F32)
                target[block] = value.astype(BF16)
                return carry

            lax.fori_loop(0, rows // TILE, add, 0)
        if place is not None:
            out = pltpu.make_async_copy(total, results[-1].at[pl.ds(place[1], rows)], done)
            out.start()
            out.wait()

    out_shape = [jax.ShapeDtypeStruct((rows, width), BF16)] * sends
    out_specs = [pl.BlockSpec(memory_space=pltpu.VMEM)] * sends
    if place is not None:
        out_shape.append(jax.ShapeDtypeStruct((place[0], width), BF16))
        out_specs.append(pl.BlockSpec(memory_space=pl.ANY))
    return pl.pallas_call(
        kernel,
        out_shape=out_shape,
        in_specs=[pl.BlockSpec(memory_space=pl.ANY)] * (sources + len(extra)),
        out_specs=out_specs,
        scratch_shapes=[
            pltpu.VMEM((len(flat), rows, width), BF16),
            pltpu.VMEM((rows, width), BF16),
            pltpu.SemaphoreType.DMA((len(flat),)),
            pltpu.SemaphoreType.DMA,
        ],
        input_output_aliases={sources + len(extra) - 1: len(sums) - 1} if feature is not None else {},
        compiler_params=pltpu.CompilerParams(vmem_limit_bytes=16 * 2**20),
        cost_estimate=pl.CostEstimate(
            flops=len(flat) * rows * width,
            bytes_accessed=(len(flat) + len(sums)) * rows * width * 2,
            transcendentals=0,
        ),
    )(*arrays, *extra)


def chained(n, cuts, lag=2):
    near = [(i, i ^ 1) for i in range(4)]
    far = [(i, i ^ 2) for i in range(4)]

    def shards(attention, out_proj, join_weight, cotangent, loss_mask):
        layers, block, _ = attention.shape
        rows, all_rows = block // cuts, 4 * block
        chunks = layers * 4 * cuts
        per = 4 * cuts
        order = [(level, j, q) for level in range(layers)
                 for j in ((3, 2, 1, 0) if level == layers - 1 else (0, 1, 2, 3)) for q in range(cuts)]

        def swap(x, pairs):
            return lax.ppermute(x, "dp", pairs)

        own = attention[0]
        first = [own, swap(own, near), swap(own, far), None]
        first[3] = swap(first[2], near)
        masked = cotangent * loss_mask[:, None].astype(BF16)
        pack = jnp.concatenate([attention[1:], masked[None]], axis=0)
        pack_far = swap(tie(pack, first[2]), far)
        packs = [pack, swap(tie(pack, first[1]), near), pack_far, swap(pack_far, near)]

        blocks = {}
        features = [None] * layers
        gradient = [None] * layers
        joined = {}
        late = {}

        def project(level, js, after):
            if level == 0:
                tokens = [first[j] for j in js]
            else:
                tokens = [packs[j][level - 1] for j in js]
            tokens = tokens[0] if len(js) == 1 else jnp.concatenate(tokens, axis=0)
            out = dot(tie(tokens, *after), out_proj[level]).astype(BF16)
            for i, j in enumerate(js):
                blocks[level, j] = (out, i * block)
            return out

        def join(level, js, after):
            lo, hi = js[0] * block, (js[-1] + 1) * block
            term = dot(tie(features[level][lo:hi], *after), join_weight[level])
            if level > 0:
                term = term + joined["sum"][lo:hi]
            if level < layers - 1:
                joined["sum"] = term
            else:
                joined[js[0]] = term
            return term

        def grad(level, after):
            if "masked" not in late:
                late["masked"] = jnp.concatenate([p[-1] for p in packs], axis=0)
            gradient[level] = lax.dot_general(
                tie(features[level], *after), late["masked"], (((0,), (0,)), ((), ())), preferred_element_type=F32
            ).astype(BF16)
            return gradient[level]

        every = (0, 1, 2, 3)
        reach = lag * (n - 1)
        work = {}

        def plan(slot, item):
            work.setdefault(slot, []).append(item)

        plan(0, lambda a: project(0, (1,), a))
        plan(2, lambda a: project(0, (2, 3), a))
        for level in range(1, layers):
            pair = ((3, 2), (1, 0)) if level == layers - 1 else ((0, 1), (2, 3))
            plan(level * per - 3, lambda a, level=level, js=pair[0]: project(level, js, a))
            plan(level * per, lambda a, level=level, js=pair[1]: project(level, js, a))
        for level in range(layers - 1):
            end = (level + 1) * per - 1 + reach
            plan(end, lambda a, level=level: join(level, every, a))
            plan(end + 1, lambda a, level=level: grad(level, a))
        level = layers - 1

        def send_back(j):
            if j == 3:
                joined["beside3"] = swap(joined[3].astype(BF16), near)
                return joined["beside3"]
            if j == 2:
                across = joined[2] + joined["beside3"].astype(F32)
                joined["across"] = swap(across.astype(BF16), far)
            if j == 1:
                joined["beside1"] = swap(joined[1].astype(BF16), near)
            return None

        for i, j in enumerate((3, 2, 1)):
            end = level * per + (i + 1) * cuts - 1 + reach
            plan(end + 1, lambda a, j=j: join(level, (j,), a))

        project(0, (0,), ())
        right, left = {}, {}
        after = []
        for k in range(chunks + reach):
            valid = [s for s in range(n - 1) if 0 <= k - lag * s < chunks]
            sums, place = [], None

            def chunk(c):
                level, j, q = order[c]
                array, row = blocks[level, j]
                return array, row + q * rows

            if valid:
                def pick(s):
                    return chunk(k - lag * (s if s in valid else valid[0]))

                for index, got in ((lambda z: z, right), (lambda z: n - 1 - z, left)):
                    terms = [[pick(index(z)) for z in range(n)]]
                    if k >= lag:
                        terms.append([(got[k - lag], 0)] * n)
                    sums.append(terms)
            c = k - reach
            if c >= 0:
                level, j, q = order[c]
                place = (all_rows, j * block + q * rows)
                sums.append([
                    [chunk(c)] * n,
                    [(right[c + lag * max(z - 1, 0)], 0) for z in range(n)],
                    [(left[c + lag * max(n - 2 - z, 0)], 0) for z in range(n)],
                ])
            got = slot_sums(n, rows, sums, place, features[level] if c >= 0 else None, after)
            if c >= 0:
                features[level] = got[-1]
            if valid:
                right[k] = lax.ppermute(got[0], "tensor", [(s, s + 1) for s in valid])
                left[k] = lax.ppermute(got[1], "tensor", [(n - 1 - s, n - 2 - s) for s in valid])
            after = [item([got[0]]) for item in work.get(k, [])]
            for j in (3, 2, 1):
                if j in joined and ("sent", j) not in joined:
                    joined["sent", j] = True
                    send_back(j)
        last = layers - 1
        join(last, (0,), ())
        out = joined[0] + joined["beside1"].astype(F32) + joined["across"].astype(F32)
        grad(last, (joined[0],))
        return (out.astype(BF16), jnp.stack(gradient, axis=0))

    return shards


def solution(mesh):
    placed = (
        P(None, ("groups", "dp"), "tensor"),
        P(None, "tensor", "dp"),
        P(None, "dp", "tensor"),
        P(("groups", "dp"), "tensor"),
        P(("groups", "dp")),
    )
    n = mesh.shape["tensor"]
    body = chained(n, 2) if mesh.shape["dp"] == 4 and n == 4 else plain
    return jax.shard_map(
        body,
        mesh=mesh,
        in_specs=placed,
        out_specs=(P(("groups", "dp"), "tensor"), P("groups", "dp", "tensor")),
        check_vma=False,
    )
```

```python
import jax
import jax.numpy as jnp
from jax import lax
from jax.experimental import pallas as pl
from jax.experimental.pallas import tpu as pltpu
from jax.sharding import PartitionSpec as P

F32 = jnp.float32
BF16 = jnp.bfloat16
TILE = 16
LIGHT = pl.CostEstimate(flops=1, bytes_accessed=1, transcendentals=0)


def plain(attention, out_proj, join_weight, cotangent, loss_mask):
    partial_value = jnp.einsum(
        "lrk,lkc->rlc",
        lax.all_gather(attention, "dp", axis=1, tiled=True),
        out_proj,
        preferred_element_type=F32,
    )
    masked = cotangent * loss_mask[:, None].astype(BF16)
    cotangent_all = lax.all_gather(masked, "dp", axis=0, tiled=True)
    summed = lax.psum(partial_value.astype(BF16), "tensor")
    joined_part = jnp.einsum("rlf,lfc->rc", summed, join_weight, preferred_element_type=F32)
    gradient = jnp.einsum("rlf,rc->lfc", summed, cotangent_all, preferred_element_type=F32)
    joined_out = lax.psum_scatter(joined_part.astype(BF16), "dp", scatter_dimension=0, tiled=True)
    return (joined_out, gradient.astype(BF16))


def rows_by_weight(pieces, rows, weight, level, add=None, kind=BF16, tile=512):
    depth, width = weight.shape[1:]
    count = len(pieces)
    total = count * rows
    arrays = []
    for array, _ in pieces:
        if not any(array is other for other in arrays):
            arrays.append(array)
    spot = [next(i for i, other in enumerate(arrays) if other is array) for array, _ in pieces]

    def kernel(*refs):
        given, w_ref = refs[: len(arrays)], refs[len(arrays)]
        o_ref, held, sems = refs[-3:]

        @pl.when(pl.program_id(0) == 0)
        def _():
            dp = lax.axis_index("dp")
            copies = [
                pltpu.make_async_copy(given[spot[i]].at[pieces[i][1](dp)], held.at[pl.ds(i * rows, rows)], sems.at[i])
                for i in range(count)
            ]
            for copy in copies:
                copy.start()
            for copy in copies:
                copy.wait()

        value = jnp.dot(held[...], w_ref[0], preferred_element_type=F32)
        if add is not None:
            value = value + refs[len(arrays) + 1][...]
        o_ref[...] = value.astype(kind)

    wide = jnp.dtype(kind).itemsize
    need = 2 * depth * (total + 2 * tile) + total * tile * (2 * wide + 4 + (8 if add is not None else 0))
    in_specs = [pl.BlockSpec(memory_space=pl.ANY)] * len(arrays)
    in_specs.append(pl.BlockSpec((1, depth, tile), lambda i: (level, 0, i)))
    given = [*arrays, weight]
    if add is not None:
        in_specs.append(pl.BlockSpec((total, tile), lambda i: (add[1], i)))
        given.append(add[0])
    return pl.pallas_call(
        kernel,
        grid=(width // tile,),
        in_specs=in_specs,
        out_specs=pl.BlockSpec((total, tile), lambda i: (0, i)),
        out_shape=jax.ShapeDtypeStruct((total, width), kind),
        scratch_shapes=[pltpu.VMEM((total, depth), BF16), pltpu.SemaphoreType.DMA((count,))],
        compiler_params=pltpu.CompilerParams(vmem_limit_bytes=max(need, 28 * 2**20) + 2 * 2**20),
        cost_estimate=LIGHT,
    )(*given)


def tie(x, *after):
    return lax.optimization_barrier((x, *after))[0]


def slot_sums(n, rows, sums, place, feature):
    arrays, where = [], {}

    def number(array):
        if id(array) not in where:
            where[id(array)] = len(arrays)
            arrays.append(array)
        return where[id(array)]

    terms = [[[(number(a), row) for a, row in term] for term in one] for one in sums]
    width = arrays[0].shape[1]
    flat = [term for one in terms for term in one]
    sources = len(arrays)
    extra = [feature] if feature is not None else []
    sends = len(sums) - (place is not None)

    def kernel(*refs):
        given = refs[:sources]
        results = refs[sources + len(extra) : sources + len(extra) + len(sums)]
        held, total, sems, done = refs[sources + len(extra) + len(sums) :]
        me = lax.axis_index("tensor") * 2 + lax.rem(lax.axis_index("dp"), 2)

        def copy(t, pick):
            array, row = pick
            return pltpu.make_async_copy(given[array].at[pl.ds(row, rows)], held.at[t], sems.at[t])

        for t, term in enumerate(flat):
            if len(set(term)) == 1:
                copy(t, term[0]).start()
        for v in range(2 * n):

            @pl.when(me == v)
            def _(v=v):
                for t, term in enumerate(flat):
                    if len(set(term)) > 1:
                        copy(t, term[v]).start()

        t = 0
        for index, one in enumerate(terms):
            used = list(range(t, t + len(one)))
            t += len(one)
            for u in used:
                copy(u, flat[u][0]).wait()
            target = total if index == sends else results[index]

            def add(i, carry, used=used, target=target):
                block = pl.ds(pl.multiple_of(i * TILE, TILE), TILE)
                value = held[used[0], block].astype(F32)
                for u in used[1:]:
                    value = value + held[u, block].astype(F32)
                target[block] = value.astype(BF16)
                return carry

            lax.fori_loop(0, rows // TILE, add, 0)
        if place is not None:
            out = pltpu.make_async_copy(total, results[-1].at[pl.ds(place[1], rows)], done)
            out.start()
            out.wait()

    out_shape = [jax.ShapeDtypeStruct((rows, width), BF16)] * sends
    out_specs = [pl.BlockSpec(memory_space=pltpu.VMEM)] * sends
    if place is not None:
        out_shape.append(jax.ShapeDtypeStruct((place[0], width), BF16))
        out_specs.append(pl.BlockSpec(memory_space=pl.ANY))
    return pl.pallas_call(
        kernel,
        out_shape=out_shape,
        in_specs=[pl.BlockSpec(memory_space=pl.ANY)] * sources + [pl.BlockSpec(memory_space=pl.ANY)] * len(extra),
        out_specs=out_specs,
        scratch_shapes=[
            pltpu.VMEM((len(flat), rows, width), BF16),
            pltpu.VMEM((rows, width), BF16),
            pltpu.SemaphoreType.DMA((len(flat),)),
            pltpu.SemaphoreType.DMA,
        ],
        input_output_aliases={sources: len(sums) - 1} if feature is not None else {},
        compiler_params=pltpu.CompilerParams(vmem_limit_bytes=8 * 2**20),
        cost_estimate=LIGHT,
    )(*arrays, *extra)


def write_gradient(features, masked, whole, level, layers, tile=256):
    tokens, depth = features.shape
    width = masked.shape[1]

    def kernel(f_ref, m_ref, *rest):
        value = lax.dot_general(f_ref[...], m_ref[...], (((0,), (0,)), ((), ())), preferred_element_type=F32)
        rest[-1][0] = value.astype(BF16)

    given = [] if whole is None else [whole]
    return pl.pallas_call(
        kernel,
        grid=(depth // tile,),
        in_specs=[
            pl.BlockSpec((tokens, tile), lambda i: (0, i)),
            pl.BlockSpec((tokens, width), lambda i: (0, 0), pipeline_mode=pl.Buffered(1)),
        ]
        + [pl.BlockSpec(memory_space=pl.ANY)] * len(given),
        out_specs=pl.BlockSpec((1, tile, width), lambda i: (level, i, 0)),
        out_shape=jax.ShapeDtypeStruct((layers, depth, width), BF16),
        input_output_aliases={2: 0} if given else {},
        compiler_params=pltpu.CompilerParams(vmem_limit_bytes=14 * 2**20),
        cost_estimate=LIGHT,
    )(features, masked, *given)


def chained(n, cuts, lag=2):
    near = [(i, i ^ 1) for i in range(4)]
    far = [(i, i ^ 2) for i in range(4)]

    def swap(x, pairs):
        return lax.ppermute(x, "dp", pairs)

    def shards(attention, out_proj, join_weight, cotangent, loss_mask):
        layers, block, _ = attention.shape
        rows, all_rows = block // cuts, 4 * block
        pairs = [(0, 0), (0, 1), (1, 0), (1, 1), (2, 1), (0, 2), (0, 3), (1, 2), (1, 3), (2, 3), (2, 2), (2, 0)]
        order = [(level, j, q) for level, j in pairs for q in range(cuts)]
        chunks = len(order)
        reach = lag * (n - 1)
        last = layers - 1

        beside = swap(attention, near)
        gathered = lax.all_gather(attention, "dp", axis=1, tiled=True)
        masked = cotangent * loss_mask[:, None].astype(BF16)
        zeros = jnp.zeros((rows, attention.shape[2]), BF16)

        def tokens(level, j, after):
            if j < 2:
                return tie(beside if j else attention, *after), lambda dp: level
            start = (level, (lax.axis_index("dp") ^ j) * block, 0)
            piece = lax.dynamic_slice(tie(gathered, *after), start, (1, block, attention.shape[2]))
            return piece, lambda dp: 0

        blocks, joined, mask = {}, {}, {}
        features, gradient = [None] * layers, [None]

        def project(level, js, after=()):
            pieces = [tokens(level, j, after) for j in js]
            if len(js) == 1:
                out = jnp.dot(pieces[0][0][level], out_proj[level], preferred_element_type=F32).astype(BF16)
            else:
                out = rows_by_weight(pieces, block, out_proj, level)
            for i, j in enumerate(js):
                blocks[level, j] = (out, i * block)
            return out

        def gather_mask(after):
            mask["gathered"] = lax.all_gather(tie(masked, *after), "dp", axis=0, tiled=True)

        def mask_all(after):
            gathered_mask = tie(mask["gathered"], *after)
            dp = lax.axis_index("dp")
            mask["all"] = jnp.concatenate(
                [lax.dynamic_slice_in_dim(gathered_mask, (dp ^ j) * block, block, axis=0) for j in range(4)], axis=0
            )
            return mask["all"]

        def join(level, js, after=()):
            place = slice(js[0] * block, (js[-1] + 1) * block)
            size = len(js) * block
            pieces = [(tie(features[level], *after), lambda dp: pl.ds(js[0] * block, size))]
            half = "low" if js[0] < 2 else "high"
            add = None if level == 0 else (joined[half], js[0] % 2)
            term = rows_by_weight(pieces, size, join_weight, level, add, F32)
            if level < last:
                joined[half] = term
            else:
                for i, j in enumerate(js):
                    joined[j] = term[i * block : (i + 1) * block]
            return term

        def grad(level, after=()):
            gradient[0] = write_gradient(tie(features[level], *after), mask["all"], gradient[0], level, layers)
            return gradient[0]

        def send_beyond(after):
            mask["beyond"] = swap(joined[3].astype(BF16), near)
            return mask["beyond"]

        def send_across(after):
            across = (joined[2] + tie(mask["beyond"], *after).astype(F32)).astype(BF16)
            mask["out"] = swap(across, far)
            return across

        def send_beside(after):
            mask["beside"] = swap(tie(joined[1], *after).astype(BF16), near)
            return mask["beside"]

        work = {
            0: [lambda a: project(0, (1,), a)],
            2: [lambda a: project(1, (0, 1), a)],
            5: [lambda a: project(2, (1, 0), a)],
            7: [lambda a: project(0, (2, 3), a)],
            8: [gather_mask],
            9: [lambda a: join(0, (0, 1), a)],
            11: [lambda a: project(1, (2, 3), a)],
            13: [lambda a: join(1, (0, 1), a)],
            15: [lambda a: project(2, (3, 2), a)],
            16: [lambda a: join(2, (1,), a)],
            17: [send_beside],
            18: [mask_all],
            19: [lambda a: join(0, (2, 3), a)],
            21: [lambda a: grad(0, a)],
            23: [lambda a: join(1, (2, 3), a)],
            25: [lambda a: grad(1, a)],
            27: [lambda a: join(2, (2, 3), a)],
            28: [send_beyond],
            29: [send_across],
        }

        project(0, (0,))
        sent = [{}, {}]
        places = [(v // 2, v % 2) for v in range(2 * n)]

        def ring(valid, turned):
            hops = []
            for d in range(4):
                rightward = (d % 2 == 0) != turned
                for s in valid:
                    z = s if rightward else n - 1 - s
                    hops.append((z * 4 + d, (z + 1 if rightward else z - 1) * 4 + d))
                if len(valid) == n - 1:
                    z = n - 1 if rightward else 0
                    hops.append((z * 4 + d, z * 4 + (d ^ 1)))
            return hops

        def came(slot, core, rightward):
            return sent[core if rightward else 1 - core][slot], 0

        after = []
        for k in range(chunks + reach):
            valid = [s for s in range(n - 1) if 0 <= k - lag * s < chunks]
            sums, place = [], None
            if 0 < k < lag:
                level, j, _ = order[k]
                blocks[level, j] = (tie(blocks[level, j][0], got[0]), blocks[level, j][1])
            if after and k - lag in sent[0]:
                sent[0][k - lag], sent[1][k - lag] = lax.optimization_barrier(
                    (sent[0][k - lag], sent[1][k - lag], *after)
                )[:2]

            def chunk(c):
                level, j, q = order[c]
                array, row = blocks[level, j]
                return array, row + q * rows

            if valid:
                for turned in (False, True):
                    first, second = [], []
                    for z, core in places:
                        rightward = (core == 0) != turned
                        s = z if rightward else n - 1 - z
                        first.append(chunk(k - lag * (s if s in valid else valid[0])))
                        if k >= lag:
                            second.append(came(k - lag, core, rightward) if s > 0 else (zeros, 0))
                    sums.append([first, second] if second else [first])
            c = k - reach
            if c >= 0:
                level, j, q = order[c]
                place = (all_rows, j * block + q * rows)
                sums.append([
                    [chunk(c)] * (2 * n),
                    [came(c + lag * (z - 1), core, True) if z > 0 else (zeros, 0) for z, core in places],
                    [came(c + lag * (n - 2 - z), core, False) if z < n - 1 else (zeros, 0) for z, core in places],
                ])
            got = slot_sums(n, rows, sums, place, features[level] if c >= 0 else None)
            if c >= 0:
                features[level] = got[-1]
            if valid:
                for turned in (False, True):
                    sent[turned][k] = lax.ppermute(got[turned], ("tensor", "dp"), ring(valid, turned))
            after = [x for x in [item([got[0]]) for item in work.get(k, [])] if x is not None]
        term = join(last, (0,), after)
        grad(last, (term,))
        out = term + mask["beside"].astype(F32) + tie(mask["out"], gradient[0]).astype(F32)
        return (out.astype(BF16), gradient[0])

    return shards


def solution(mesh):
    placed = (
        P(None, ("groups", "dp"), "tensor"),
        P(None, "tensor", "dp"),
        P(None, "dp", "tensor"),
        P(("groups", "dp"), "tensor"),
        P(("groups", "dp")),
    )
    n = mesh.shape["tensor"]
    body = chained(n, 2) if mesh.shape["dp"] == 4 and n == 4 else plain
    return jax.shard_map(
        body,
        mesh=mesh,
        in_specs=placed,
        out_specs=(P(("groups", "dp"), "tensor"), P("groups", "dp", "tensor")),
        check_vma=False,
    )
```

```python
import jax
import jax.numpy as jnp
from jax import lax
from jax.experimental import pallas as pl
from jax.experimental.pallas import tpu as pltpu
from jax.sharding import PartitionSpec as P

F32 = jnp.float32
BF16 = jnp.bfloat16
TILE = 16
DEEP = 2**14
LIGHT = pl.CostEstimate(flops=1, bytes_accessed=1, transcendentals=0)


def plain(attention, out_proj, join_weight, cotangent, loss_mask):
    partial_value = jnp.einsum(
        "lrk,lkc->rlc",
        lax.all_gather(attention, "dp", axis=1, tiled=True),
        out_proj,
        preferred_element_type=F32,
    )
    masked = cotangent * loss_mask[:, None].astype(BF16)
    cotangent_all = lax.all_gather(masked, "dp", axis=0, tiled=True)
    summed = lax.psum(partial_value.astype(BF16), "tensor")
    joined_part = jnp.einsum("rlf,lfc->rc", summed, join_weight, preferred_element_type=F32)
    gradient = jnp.einsum("rlf,rc->lfc", summed, cotangent_all, preferred_element_type=F32)
    joined_out = lax.psum_scatter(joined_part.astype(BF16), "dp", scatter_dimension=0, tiled=True)
    return (joined_out, gradient.astype(BF16))


def rows_by_weight(store, pieces, rows, weight, level, target=None, add=None, tile=512):
    depth, width = weight.shape[1:]
    count = len(pieces)
    total = count * rows
    given = [weight] + ([add[0]] if add is not None else []) + [array for array, _ in pieces if array is not None]
    own = target is None
    began = store is not None

    def kernel(*refs):
        refs = list(refs)
        w_ref = refs.pop(0)
        add_ref = refs.pop(0) if add is not None else None
        sources = [refs.pop(0) if array is not None else None for array, _ in pieces]
        if began:
            refs.pop(0)
        store_ref = refs.pop(0)
        o_ref = refs.pop(0) if own else None
        held, ready, sems, done = refs
        step = pl.program_id(0)

        @pl.when(step == 0)
        def _():
            copies = [
                pltpu.make_async_copy(
                    (store_ref if source is None else source).at[index], held.at[pl.ds(i * rows, rows)], sems.at[i]
                )
                for i, (source, (_, index)) in enumerate(zip(sources, pieces))
            ]
            for copy in copies:
                copy.start()
            for copy in copies:
                copy.wait()

        value = jnp.dot(held[...], w_ref[0], preferred_element_type=F32)
        if add is not None:
            value = value + add_ref[...]
        if own:
            o_ref[...] = value
        else:

            def put(i):
                columns = pl.ds(pl.multiple_of(i * tile, tile), tile)
                return pltpu.make_async_copy(ready, store_ref.at[pl.ds(target, total), columns], done)

            @pl.when(step > 0)
            def _():
                put(step - 1).wait()

            ready[...] = value.astype(BF16)
            put(step).start()

            @pl.when(step == width // tile - 1)
            def _():
                put(step).wait()

    in_specs = [pl.BlockSpec((1, depth, tile), lambda i: (level, 0, i))]
    if add is not None:
        in_specs.append(pl.BlockSpec((total, tile), lambda i: (add[1], i)))
    in_specs += [pl.BlockSpec(memory_space=pl.ANY)] * (len(given) - len(in_specs) + began)
    out_shape = [jax.ShapeDtypeStruct((DEEP, width), BF16)]
    out_specs = [pl.BlockSpec(memory_space=pl.ANY)]
    if own:
        out_shape.append(jax.ShapeDtypeStruct((total, width), F32))
        out_specs.append(pl.BlockSpec((total, tile), lambda i: (0, i)))
    got = pl.pallas_call(
        kernel,
        grid=(width // tile,),
        in_specs=in_specs,
        out_specs=out_specs,
        out_shape=out_shape,
        input_output_aliases={len(given): 0} if began else {},
        scratch_shapes=[
            pltpu.VMEM((total, depth), BF16),
            pltpu.VMEM((TILE, 128) if own else (total, tile), BF16),
            pltpu.SemaphoreType.DMA((count,)),
            pltpu.SemaphoreType.DMA,
        ],
        compiler_params=pltpu.CompilerParams(vmem_limit_bytes=38 * 2**20),
        cost_estimate=LIGHT,
    )(*given, *([store] if began else []))
    return got[0], got[1] if own else None


def tie(x, *after):
    return lax.optimization_barrier((x, *after))[0]


def slot_sums(store, n, rows, sums, place):
    arrays, where = [], {}

    def number(array):
        if array is None:
            return -1
        if id(array) not in where:
            where[id(array)] = len(arrays)
            arrays.append(array)
        return where[id(array)]

    terms = [[[(number(a), row) for a, row in term] for term in one] for one in sums]
    width = store.shape[1]
    flat = [term for one in terms for term in one]
    sends = len(sums) - (place is not None)

    def kernel(*refs):
        given = refs[: len(arrays)]
        store_ref = refs[len(arrays) + 1]
        results = refs[len(arrays) + 2 : len(arrays) + 2 + sends]
        held, total, sems, done = refs[len(arrays) + 2 + sends :]
        me = lax.axis_index("tensor") * 2 + lax.rem(lax.axis_index("dp"), 2)

        def copy(t, pick):
            array, row = pick
            source = store_ref if array < 0 else given[array]
            return pltpu.make_async_copy(source.at[pl.ds(row, rows)], held.at[t], sems.at[t])

        for t, term in enumerate(flat):
            if len(set(term)) == 1:
                copy(t, term[0]).start()
        for v in range(2 * n):

            @pl.when(me == v)
            def _(v=v):
                for t, term in enumerate(flat):
                    if len(set(term)) > 1:
                        copy(t, term[v]).start()

        first = [sum(len(one) for one in terms[:index]) for index in range(len(terms))]
        out = None
        for index in reversed(range(len(terms))):
            used = range(first[index], first[index] + len(terms[index]))
            for u in used:
                copy(u, flat[u][0]).wait()
            target = total if index == sends else results[index]

            def add(i, carry, used=used, target=target):
                block = pl.ds(pl.multiple_of(i * TILE, TILE), TILE)
                value = held[used[0], block].astype(F32)
                for u in used[1:]:
                    value = value + held[u, block].astype(F32)
                target[block] = value.astype(BF16)
                return carry

            lax.fori_loop(0, rows // TILE, add, 0)
            if index == sends:
                out = pltpu.make_async_copy(total, store_ref.at[pl.ds(place, rows)], done)
                out.start()
        if out is not None:
            out.wait()

    got = pl.pallas_call(
        kernel,
        out_shape=[jax.ShapeDtypeStruct(store.shape, BF16)] + [jax.ShapeDtypeStruct((rows, width), BF16)] * sends,
        in_specs=[pl.BlockSpec(memory_space=pl.ANY)] * (len(arrays) + 1),
        out_specs=[pl.BlockSpec(memory_space=pl.ANY)] + [pl.BlockSpec(memory_space=pltpu.VMEM)] * sends,
        scratch_shapes=[
            pltpu.VMEM((len(flat), rows, width), BF16),
            pltpu.VMEM((rows, width), BF16),
            pltpu.SemaphoreType.DMA((len(flat),)),
            pltpu.SemaphoreType.DMA,
        ],
        input_output_aliases={len(arrays): 0},
        compiler_params=pltpu.CompilerParams(vmem_limit_bytes=8 * 2**20),
        cost_estimate=LIGHT,
    )(*arrays, store)
    return got[0], got[1:]


def write_gradient(store, row, masked, whole, level, layers, tile=256):
    tokens, width = masked.shape
    depth = store.shape[1]

    def kernel(m_ref, *rest):
        store_ref, o_ref, held, sem = rest[-4:]

        @pl.when(pl.program_id(0) == 0)
        def _():
            copy = pltpu.make_async_copy(store_ref.at[pl.ds(row, tokens)], held, sem)
            copy.start()
            copy.wait()

        columns = pl.ds(pl.multiple_of(pl.program_id(0) * tile, tile), tile)
        value = lax.dot_general(held[:, columns], m_ref[...], (((0,), (0,)), ((), ())), preferred_element_type=F32)
        o_ref[0] = value.astype(BF16)

    given = [store] if whole is None else [store, whole]
    return pl.pallas_call(
        kernel,
        grid=(depth // tile,),
        in_specs=[pl.BlockSpec((tokens, width), lambda i: (0, 0), pipeline_mode=pl.Buffered(1))]
        + [pl.BlockSpec(memory_space=pl.ANY)] * len(given),
        out_specs=[
            pl.BlockSpec(memory_space=pl.ANY),
            pl.BlockSpec((1, tile, width), lambda i: (level, i, 0)),
        ],
        out_shape=[
            jax.ShapeDtypeStruct(store.shape, BF16),
            jax.ShapeDtypeStruct((layers, depth, width), BF16),
        ],
        scratch_shapes=[pltpu.VMEM((tokens, depth), BF16), pltpu.SemaphoreType.DMA],
        input_output_aliases={1: 0} if whole is None else {1: 0, 2: 1},
        compiler_params=pltpu.CompilerParams(vmem_limit_bytes=18 * 2**20),
        cost_estimate=LIGHT,
    )(masked, *given)


def chained(n, cuts, lag=2):
    near = [(i, i ^ 1) for i in range(4)]
    far = [(i, i ^ 2) for i in range(4)]

    def swap(x, pairs):
        return lax.ppermute(x, "dp", pairs)

    def shards(attention, out_proj, join_weight, cotangent, loss_mask):
        layers, block, _ = attention.shape
        rows = block // cuts
        pairs = [(0, 0), (0, 1), (1, 0), (1, 1), (0, 2), (0, 3), (1, 2), (1, 3), (2, 1), (2, 3), (2, 2), (2, 0)]
        order = [(level, j, q) for level, j in pairs for q in range(cuts)]
        chunks = len(order)
        reach = lag * (n - 1)
        last = layers - 1

        beside = swap(attention, near)
        gathered = lax.all_gather(attention, "dp", axis=1, tiled=True)
        zeros = jnp.zeros((rows, attention.shape[2]), BF16)

        def tokens(level, j, after):
            if j < 2:
                return tie(beside if j else attention, *after), level
            start = (level, (lax.axis_index("dp") ^ j) * block, 0)
            return lax.dynamic_slice(tie(gathered, *after), start, (1, block, attention.shape[2])), 0

        joined, mask = {}, {}
        store, gradient = [None], [None]

        def partial_row(level, j):
            return (level * 4 + (3 - j if level == last else j)) * block

        def feature_row(level, j):
            return (layers * 4 + level * 4 + j) * block


        def project(level, js, after=()):
            pieces = [tokens(level, j, after) for j in js]
            store[0], _ = rows_by_weight(store[0], pieces, block, out_proj, level, partial_row(level, js[0]))

        def mask_far(after):
            mask["own"] = tie(cotangent, *after) * loss_mask[:, None].astype(BF16)
            mask["far"] = swap(mask["own"], far)

        def mask_near(after):
            both = jnp.stack([mask["own"], tie(mask["far"], *after)])
            mask["both"] = both, swap(both, near)

        def mask_all(after):
            here, beside_it = mask["both"][0], tie(mask["both"][1], *after)
            mask["all"] = jnp.concatenate([here[0], beside_it[0], here[1], beside_it[1]], axis=0)
            return mask["all"]

        def join(level, js, after=()):
            size = len(js) * block
            half = "low" if js[0] < 2 else "high"
            add = None if level == 0 else (joined[half], js[0] % 2)
            pieces = [(None, pl.ds(feature_row(level, js[0]), size))]
            store[0], term = rows_by_weight(store[0], pieces, size, join_weight, level, None, add)
            if level < last:
                joined[half] = term
            else:
                for i, j in enumerate(js):
                    joined[j] = term[i * block : (i + 1) * block]
            return term

        def grad(level, after=()):
            store[0], gradient[0] = write_gradient(
                store[0], feature_row(level, 0), mask["all"], gradient[0], level, layers
            )

        def send_near():
            both = jnp.stack([joined[1], joined[3]]).astype(BF16)
            mask["beside"] = swap(tie(both, sent[0][chunks + lag * (n - 2) - 2]), near)

        work = {
            1: [lambda a: project(0, (1,), a)],
            2: [lambda a: project(1, (0, 1), a)],
            7: [lambda a: project(0, (2, 3), a)],
            9: [lambda a: join(0, (0, 1), a)],
            10: [lambda a: project(1, (2, 3), a), mask_far],
            12: [lambda a: project(2, (1, 0), a)],
            13: [mask_near],
            14: [lambda a: join(1, (0, 1), a)],
            15: [lambda a: project(2, (3, 2), a)],
            16: [mask_all],
            17: [lambda a: join(0, (2, 3), a)],
            18: [lambda a: grad(0, a)],
            21: [lambda a: join(1, (2, 3), a)],
            22: [lambda a: grad(1, a)],
            24: [lambda a: join(2, (1,), a)],
            26: [lambda a: join(2, (3,), a)],
        }

        project(0, (0,))
        sent = [{}, {}]
        places = [(v // 2, v % 2) for v in range(2 * n)]

        def ring(valid, turned):
            hops = []
            for d in range(4):
                rightward = (d % 2 == 0) != turned
                for s in valid:
                    z = s if rightward else n - 1 - s
                    hops.append((z * 4 + d, (z + 1 if rightward else z - 1) * 4 + d))
                if len(valid) == n - 1:
                    z = n - 1 if rightward else 0
                    hops.append((z * 4 + d, z * 4 + (d ^ 1)))
            return hops

        def came(slot, core, rightward):
            return sent[core if rightward else 1 - core][slot], 0

        after = []
        for k in range(chunks + reach):
            valid = [s for s in range(n - 1) if 0 <= k - lag * s < chunks]
            sums, place = [], None
            if after and k - lag in sent[0]:
                sent[0][k - lag], sent[1][k - lag] = lax.optimization_barrier(
                    (sent[0][k - lag], sent[1][k - lag], *after)
                )[:2]

            def chunk(c):
                level, j, q = order[c]
                return None, partial_row(level, j) + q * rows

            if valid:
                for turned in (False, True):
                    first, second = [], []
                    for z, core in places:
                        rightward = (core == 0) != turned
                        s = z if rightward else n - 1 - z
                        first.append(chunk(k - lag * (s if s in valid else valid[0])))
                        if k >= lag:
                            second.append(came(k - lag, core, rightward) if s > 0 else (zeros, 0))
                    sums.append([first, second] if second else [first])
            c = k - reach
            if c >= 0:
                level, j, q = order[c]
                place = feature_row(level, j) + q * rows
                sums.append([
                    [chunk(c)] * (2 * n),
                    [came(c + lag * (z - 1), core, True) if z > 0 else (zeros, 0) for z, core in places],
                    [came(c + lag * (n - 2 - z), core, False) if z < n - 1 else (zeros, 0) for z, core in places],
                ])
            store[0], got = slot_sums(store[0], n, rows, sums, place)
            if valid:
                for turned in (False, True):
                    sent[turned][k] = lax.ppermute(got[turned], ("tensor", "dp"), ring(valid, turned))
            after = [x for x in [item(list(got[:1])) for item in work.get(k, [])] if x is not None]
        send_near()
        across = join(last, (2,)) + mask["beside"][1].astype(F32)
        across = swap(across.astype(BF16), far)
        term = join(last, (0,))
        grad(last)
        out = term + mask["beside"][0].astype(F32) + tie(across, gradient[0]).astype(F32)
        return (out.astype(BF16), gradient[0])

    return shards


def solution(mesh):
    placed = (
        P(None, ("groups", "dp"), "tensor"),
        P(None, "tensor", "dp"),
        P(None, "dp", "tensor"),
        P(("groups", "dp"), "tensor"),
        P(("groups", "dp")),
    )
    n = mesh.shape["tensor"]
    body = chained(n, 2) if mesh.shape["dp"] == 4 and n == 4 else plain
    return jax.shard_map(
        body,
        mesh=mesh,
        in_specs=placed,
        out_specs=(P(("groups", "dp"), "tensor"), P("groups", "dp", "tensor")),
        check_vma=False,
    )
```

```python
import jax
import jax.numpy as jnp
from jax import lax
from jax.experimental import pallas as pl
from jax.experimental.pallas import tpu as pltpu
from jax.sharding import PartitionSpec as P

F32 = jnp.float32
BF16 = jnp.bfloat16
TILE = 16
DEEP = 2**14
LIGHT = pl.CostEstimate(flops=1, bytes_accessed=1, transcendentals=0)


def plain(attention, out_proj, join_weight, cotangent, loss_mask):
    partial_value = jnp.einsum(
        "lrk,lkc->rlc",
        lax.all_gather(attention, "dp", axis=1, tiled=True),
        out_proj,
        preferred_element_type=F32,
    )
    masked = cotangent * loss_mask[:, None].astype(BF16)
    cotangent_all = lax.all_gather(masked, "dp", axis=0, tiled=True)
    summed = lax.psum(partial_value.astype(BF16), "tensor")
    joined_part = jnp.einsum("rlf,lfc->rc", summed, join_weight, preferred_element_type=F32)
    gradient = jnp.einsum("rlf,rc->lfc", summed, cotangent_all, preferred_element_type=F32)
    joined_out = lax.psum_scatter(joined_part.astype(BF16), "dp", scatter_dimension=0, tiled=True)
    return (joined_out, gradient.astype(BF16))


def rows_by_weight(store, pieces, rows, weight, level, target=None, add=None, tile=512):
    depth, width = weight.shape[1:]
    count = len(pieces)
    total = count * rows
    given = [weight] + ([add[0]] if add is not None else []) + [array for array, _ in pieces if array is not None]
    own = target is None
    began = store is not None

    def kernel(*refs):
        refs = list(refs)
        w_ref = refs.pop(0)
        add_ref = refs.pop(0) if add is not None else None
        sources = [refs.pop(0) if array is not None else None for array, _ in pieces]
        if began:
            refs.pop(0)
        store_ref = refs.pop(0)
        o_ref = refs.pop(0) if own else None
        held, ready, sems, done = refs
        step = pl.program_id(0)

        @pl.when(step == 0)
        def _():
            copies = [
                pltpu.make_async_copy(
                    (store_ref if source is None else source).at[index], held.at[pl.ds(i * rows, rows)], sems.at[i]
                )
                for i, (source, (_, index)) in enumerate(zip(sources, pieces))
            ]
            for copy in copies:
                copy.start()
            for copy in copies:
                copy.wait()

        value = jnp.dot(held[...], w_ref[0], preferred_element_type=F32)
        if add is not None:
            value = value + add_ref[...]
        if own:
            o_ref[...] = value
        else:

            def put(i):
                columns = pl.ds(pl.multiple_of(i * tile, tile), tile)
                return pltpu.make_async_copy(ready, store_ref.at[pl.ds(target, total), columns], done)

            @pl.when(step > 0)
            def _():
                put(step - 1).wait()

            ready[...] = value.astype(BF16)
            put(step).start()

            @pl.when(step == width // tile - 1)
            def _():
                put(step).wait()

    in_specs = [pl.BlockSpec((1, depth, tile), lambda i: (level, 0, i))]
    if add is not None:
        in_specs.append(pl.BlockSpec((total, tile), lambda i: (add[1], i)))
    in_specs += [pl.BlockSpec(memory_space=pl.ANY)] * (len(given) - len(in_specs) + began)
    out_shape = [jax.ShapeDtypeStruct((DEEP, width), BF16)]
    out_specs = [pl.BlockSpec(memory_space=pl.ANY)]
    if own:
        out_shape.append(jax.ShapeDtypeStruct((total, width), F32))
        out_specs.append(pl.BlockSpec((total, tile), lambda i: (0, i)))
    got = pl.pallas_call(
        kernel,
        grid=(width // tile,),
        in_specs=in_specs,
        out_specs=out_specs,
        out_shape=out_shape,
        input_output_aliases={len(given): 0} if began else {},
        scratch_shapes=[
            pltpu.VMEM((total, depth), BF16),
            pltpu.VMEM((TILE, 128) if own else (total, tile), BF16),
            pltpu.SemaphoreType.DMA((count,)),
            pltpu.SemaphoreType.DMA,
        ],
        compiler_params=pltpu.CompilerParams(vmem_limit_bytes=38 * 2**20),
        cost_estimate=LIGHT,
    )(*given, *([store] if began else []))
    return got[0], got[1] if own else None


def tie(x, *after):
    return lax.optimization_barrier((x, *after))[0]


def slot_sums(store, n, rows, sums, place):
    arrays, where = [], {}

    def number(array):
        if array is None:
            return -1
        if id(array) not in where:
            where[id(array)] = len(arrays)
            arrays.append(array)
        return where[id(array)]

    terms = [[[(number(a), row) for a, row in term] for term in one] for one in sums]
    width = store.shape[1]
    flat = [term for one in terms for term in one]
    sends = len(sums) - (place is not None)

    def kernel(*refs):
        given = refs[: len(arrays)]
        store_ref = refs[len(arrays) + 1]
        results = refs[len(arrays) + 2 : len(arrays) + 2 + sends]
        held, total, sems, done = refs[len(arrays) + 2 + sends :]
        me = lax.axis_index("tensor") * 2 + lax.rem(lax.axis_index("dp"), 2)

        def copy(t, pick):
            array, row = pick
            source = store_ref if array < 0 else given[array]
            return pltpu.make_async_copy(source.at[pl.ds(row, rows)], held.at[t], sems.at[t])

        for t, term in enumerate(flat):
            if len(set(term)) == 1:
                copy(t, term[0]).start()
        for v in range(2 * n):

            @pl.when(me == v)
            def _(v=v):
                for t, term in enumerate(flat):
                    if len(set(term)) > 1:
                        copy(t, term[v]).start()

        first = [sum(len(one) for one in terms[:index]) for index in range(len(terms))]
        out = None
        for index in reversed(range(len(terms))):
            used = range(first[index], first[index] + len(terms[index]))
            for u in used:
                copy(u, flat[u][0]).wait()
            target = total if index == sends else results[index]

            def add(i, carry, used=used, target=target):
                block = pl.ds(pl.multiple_of(i * TILE, TILE), TILE)
                value = held[used[0], block].astype(F32)
                for u in used[1:]:
                    value = value + held[u, block].astype(F32)
                target[block] = value.astype(BF16)
                return carry

            lax.fori_loop(0, rows // TILE, add, 0)
            if index == sends:
                out = pltpu.make_async_copy(total, store_ref.at[pl.ds(place, rows)], done)
                out.start()
        if out is not None:
            out.wait()

    got = pl.pallas_call(
        kernel,
        out_shape=[jax.ShapeDtypeStruct(store.shape, BF16)] + [jax.ShapeDtypeStruct((rows, width), BF16)] * sends,
        in_specs=[pl.BlockSpec(memory_space=pl.ANY)] * (len(arrays) + 1),
        out_specs=[pl.BlockSpec(memory_space=pl.ANY)] + [pl.BlockSpec(memory_space=pltpu.VMEM)] * sends,
        scratch_shapes=[
            pltpu.VMEM((len(flat), rows, width), BF16),
            pltpu.VMEM((rows, width), BF16),
            pltpu.SemaphoreType.DMA((len(flat),)),
            pltpu.SemaphoreType.DMA,
        ],
        input_output_aliases={len(arrays): 0},
        compiler_params=pltpu.CompilerParams(vmem_limit_bytes=8 * 2**20),
        cost_estimate=LIGHT,
    )(*arrays, store)
    return got[0], got[1:]


def write_gradient(store, row, masked, whole, level, layers, tile=256):
    tokens, width = masked.shape
    depth = store.shape[1]

    def kernel(m_ref, *rest):
        store_ref, o_ref, held, sem = rest[-4:]

        @pl.when(pl.program_id(0) == 0)
        def _():
            copy = pltpu.make_async_copy(store_ref.at[pl.ds(row, tokens)], held, sem)
            copy.start()
            copy.wait()

        columns = pl.ds(pl.multiple_of(pl.program_id(0) * tile, tile), tile)
        value = lax.dot_general(held[:, columns], m_ref[...], (((0,), (0,)), ((), ())), preferred_element_type=F32)
        o_ref[0] = value.astype(BF16)

    given = [store] if whole is None else [store, whole]
    return pl.pallas_call(
        kernel,
        grid=(depth // tile,),
        in_specs=[pl.BlockSpec((tokens, width), lambda i: (0, 0), pipeline_mode=pl.Buffered(1))]
        + [pl.BlockSpec(memory_space=pl.ANY)] * len(given),
        out_specs=[
            pl.BlockSpec(memory_space=pl.ANY),
            pl.BlockSpec((1, tile, width), lambda i: (level, i, 0)),
        ],
        out_shape=[
            jax.ShapeDtypeStruct(store.shape, BF16),
            jax.ShapeDtypeStruct((layers, depth, width), BF16),
        ],
        scratch_shapes=[pltpu.VMEM((tokens, depth), BF16), pltpu.SemaphoreType.DMA],
        input_output_aliases={1: 0} if whole is None else {1: 0, 2: 1},
        compiler_params=pltpu.CompilerParams(vmem_limit_bytes=18 * 2**20),
        cost_estimate=LIGHT,
    )(masked, *given)


def chained(n, cuts, lag=2):
    near = [(i, i ^ 1) for i in range(4)]
    far = [(i, i ^ 2) for i in range(4)]

    def swap(x, pairs):
        return lax.ppermute(x, "dp", pairs)

    def shards(attention, out_proj, join_weight, cotangent, loss_mask):
        layers, block, _ = attention.shape
        rows = block // cuts
        pairs = [(0, 0), (0, 1), (1, 0), (1, 1), (0, 2), (0, 3), (1, 2), (1, 3), (2, 1), (2, 3), (2, 2), (2, 0)]
        order = [(level, j, q) for level, j in pairs for q in range(cuts)]
        chunks = len(order)
        reach = lag * (n - 1)
        last = layers - 1

        beside = swap(attention, near)
        gathered = lax.all_gather(attention, "dp", axis=1, tiled=True)
        zeros = jnp.zeros((rows, attention.shape[2]), BF16)

        def tokens(level, j, after):
            if j < 2:
                return tie(beside if j else attention, *after), level
            start = (level, (lax.axis_index("dp") ^ j) * block, 0)
            return lax.dynamic_slice(tie(gathered, *after), start, (1, block, attention.shape[2])), 0

        joined, mask = {}, {}
        store, gradient = [None], [None]

        def partial_row(level, j):
            return (level * 4 + (3 - j if level == last else j)) * block

        def feature_row(level, j):
            return (layers * 4 + level * 4 + j) * block


        def project(level, js, after=()):
            pieces = [tokens(level, j, after) for j in js]
            store[0], _ = rows_by_weight(store[0], pieces, block, out_proj, level, partial_row(level, js[0]))

        def mask_far(after):
            mask["own"] = tie(cotangent, *after) * loss_mask[:, None].astype(BF16)
            mask["far"] = swap(mask["own"], far)

        def mask_near(after):
            both = jnp.stack([mask["own"], tie(mask["far"], *after)])
            mask["both"] = both, swap(both, near)

        def mask_all(after):
            here, beside_it = mask["both"][0], tie(mask["both"][1], *after)
            mask["all"] = jnp.concatenate([here[0], beside_it[0], here[1], beside_it[1]], axis=0)
            return mask["all"]

        def join(level, js, after=()):
            size = len(js) * block
            half = "low" if js[0] < 2 else "high"
            add = None if level == 0 else (joined[half], js[0] % 2)
            pieces = [(None, pl.ds(feature_row(level, js[0]), size))]
            store[0], term = rows_by_weight(store[0], pieces, size, join_weight, level, None, add)
            if level < last:
                joined[half] = term
            else:
                for i, j in enumerate(js):
                    joined[j] = term[i * block : (i + 1) * block]
            return term

        def grad(level, after=()):
            store[0], gradient[0] = write_gradient(
                store[0], feature_row(level, 0), mask["all"], gradient[0], level, layers
            )

        def send_near():
            both = jnp.stack([joined[1], joined[3]]).astype(BF16)
            mask["beside"] = swap(tie(both, sent[0][chunks + lag * (n - 2) - 2]), near)

        work = {
            1: [lambda a: project(0, (1,), a)],
            2: [lambda a: project(1, (0, 1), a)],
            7: [lambda a: project(0, (2, 3), a)],
            9: [lambda a: join(0, (0, 1), a)],
            10: [lambda a: project(1, (2, 3), a), mask_far],
            12: [lambda a: project(2, (1, 0), a)],
            13: [mask_near],
            14: [lambda a: join(1, (0, 1), a)],
            15: [lambda a: project(2, (3, 2), a)],
            16: [mask_all],
            17: [lambda a: join(0, (2, 3), a)],
            18: [lambda a: grad(0, a)],
            21: [lambda a: join(1, (2, 3), a)],
            22: [lambda a: grad(1, a)],
            24: [lambda a: join(2, (1,), a)],
            28: [lambda a: join(2, (3,), a)],
        }

        project(0, (0,))
        sent = [{}, {}]
        places = [(v // 2, v % 2) for v in range(2 * n)]

        def ring(valid, turned):
            hops = []
            for d in range(4):
                rightward = (d % 2 == 0) != turned
                for s in valid:
                    z = s if rightward else n - 1 - s
                    hops.append((z * 4 + d, (z + 1 if rightward else z - 1) * 4 + d))
                if len(valid) == n - 1:
                    z = n - 1 if rightward else 0
                    hops.append((z * 4 + d, z * 4 + (d ^ 1)))
            return hops

        def came(slot, core, rightward):
            return sent[core if rightward else 1 - core][slot], 0

        after = []
        for k in range(chunks + reach):
            valid = [s for s in range(n - 1) if 0 <= k - lag * s < chunks]
            sums, place = [], None
            if after and k - lag in sent[0]:
                sent[0][k - lag], sent[1][k - lag] = lax.optimization_barrier(
                    (sent[0][k - lag], sent[1][k - lag], *after)
                )[:2]

            def chunk(c):
                level, j, q = order[c]
                return None, partial_row(level, j) + q * rows

            if valid:
                for turned in (False, True):
                    first, second = [], []
                    for z, core in places:
                        rightward = (core == 0) != turned
                        s = z if rightward else n - 1 - z
                        first.append(chunk(k - lag * (s if s in valid else valid[0])))
                        if k >= lag:
                            second.append(came(k - lag, core, rightward) if s > 0 else (zeros, 0))
                    sums.append([first, second] if second else [first])
            c = k - reach
            if c >= 0:
                level, j, q = order[c]
                place = feature_row(level, j) + q * rows
                sums.append([
                    [chunk(c)] * (2 * n),
                    [came(c + lag * (z - 1), core, True) if z > 0 else (zeros, 0) for z, core in places],
                    [came(c + lag * (n - 2 - z), core, False) if z < n - 1 else (zeros, 0) for z, core in places],
                ])
            store[0], got = slot_sums(store[0], n, rows, sums, place)
            if valid:
                for turned in (False, True):
                    sent[turned][k] = lax.ppermute(got[turned], ("tensor", "dp"), ring(valid, turned))
            after = [x for x in [item(list(got[:1])) for item in work.get(k, [])] if x is not None]
        send_near()
        across = join(last, (2,)) + mask["beside"][1].astype(F32)
        across = swap(across.astype(BF16), far)
        term = join(last, (0,))
        grad(last)
        out = term + mask["beside"][0].astype(F32) + tie(across, gradient[0]).astype(F32)
        return (out.astype(BF16), gradient[0])

    return shards


def solution(mesh):
    placed = (
        P(None, ("groups", "dp"), "tensor"),
        P(None, "tensor", "dp"),
        P(None, "dp", "tensor"),
        P(("groups", "dp"), "tensor"),
        P(("groups", "dp")),
    )
    n = mesh.shape["tensor"]
    body = chained(n, 2) if mesh.shape["dp"] == 4 and n == 4 else plain
    return jax.shard_map(
        body,
        mesh=mesh,
        in_specs=placed,
        out_specs=(P(("groups", "dp"), "tensor"), P("groups", "dp", "tensor")),
        check_vma=False,
    )
```
